32 devices in a mesh: row: 4 (over z), col: 8 (over y, x, core).
Axes of the slice: x: 2, y: 2, z: 4, core: 2. Of those that a mesh axis runs over, the one named last changes fastest.
Arguments:
- valence: bfloat16 [32, 2, 64000], P(('row', 'col')), may hold values from -2.09375 to 2.09375
- conduction: bfloat16 [128, 2, 64000], P(('row', 'col')), may hold values from -2.09375 to 2.09375
- valence_slot_index: int32 [2], replicated, may hold values from 0 to 31
- weights: float32 [2, 128], P(None, ('row', 'col')), may hold values from 0.1 to 1
- sphere_index: int32 [9984], replicated, may hold values from 0 to 63999, as said below
Outputs:
- polarizability: float32 [2, 9984, 9984], P(None, 'row', 'col')
The draws below stay inside these ranges and needn't reach their ends.
Inputs may be any that keep to these rules, and one draw needn't show every extreme that they name: `sphere_index`: all entries are distinct.
All inputs are finite; a program needn't handle non-finite values.
Results may differ from the reference program's by a relative error of at most 0.0039.
Values may be sent and summed in bfloat16 or wider, within the bound.
A program may use at most 256 MiB of HBM per device.

```python
import math
import jax
import jax.numpy as jnp

NBOX = 40
NG = 9984
WINDOW_VALENCE = 2
GRID_POINTS = 64000
NC = 128
VALENCE_SLOTS = 32


def draw_sphere_index(key, part):
    first = jax.random.fold_in(key, 11)
    second = jax.random.fold_in(key, 23)
    inner = 1 + jax.random.permutation(first, NBOX ** 3 - 2)[:NG - 2]
    ends = jnp.array([0, NBOX ** 3 - 1], dtype=jnp.int32)
    joined = jnp.concatenate([ends, inner.astype(jnp.int32)])
    return jax.random.permutation(second, joined).astype(jnp.int32)


def shard_levels(stream_key, shape, pieces, low, high):
    factor_of, own = 1.0, jax.random.fold_in(stream_key, 6)
    for position, shards_of in pieces:
        heights = jnp.exp(jax.random.uniform(jax.random.fold_in(own, position), (shards_of,), jnp.float32, low / len(pieces), high / len(pieces)))
        factor_of = factor_of * jnp.repeat(heights, shape[position] // shards_of).reshape([-1 if axis == position else 1 for axis in range(len(shape))])
    return factor_of


def noise(key, dims, width, most, shards=(), kind=jnp.bfloat16):
    result = jax.random.normal(key, dims, jnp.float32) * width
    if len(shards) > 0:
        result = shard_levels(key, dims, shards, -0.22, 0.18) * result
    return jnp.clip(result, min=-most, max=most).astype(kind)


def setup_inputs(seed: int = 0) -> dict:
    arg_keys = jax.random.split(jax.random.key(seed), 6)
    valence = noise(arg_keys[0], (VALENCE_SLOTS, 2, GRID_POINTS), 0.35, 2.09375, ((0, 32),))
    conduction = noise(arg_keys[1], (NC, 2, GRID_POINTS), 0.35, 2.09375, ((0, 32),))
    valence_slot_index = jax.random.randint(arg_keys[2], (WINDOW_VALENCE,), 0, VALENCE_SLOTS).astype(jnp.int32)
    weights = jnp.clip(jnp.exp(math.log(1.0) - 2.3025851 * jax.random.uniform(arg_keys[3], (WINDOW_VALENCE, NC), jnp.float32) ** shard_levels(arg_keys[3], (WINDOW_VALENCE, NC), ((1, 32),), -0.2, 0.2)), 0.1, 1.0)
    sphere_index = draw_sphere_index(jax.random.fold_in(arg_keys[5], 71), 0)
    return dict(valence=valence, conduction=conduction, valence_slot_index=valence_slot_index, weights=weights, sphere_index=sphere_index)


def reference(valence, conduction, valence_slot_index, weights, sphere_index):
    chosen = valence[valence_slot_index].astype(jnp.float32)
    states = conduction.astype(jnp.float32)
    val_re = chosen[:, 0][:, None, :]
    val_im = chosen[:, 1][:, None, :]
    con_re = states[:, 0][None, :, :]
    con_im = states[:, 1][None, :, :]
    dens_re = val_re * con_re + val_im * con_im
    dens_im = val_re * con_im - val_im * con_re
    field = (dens_re + 1j * dens_im).reshape(WINDOW_VALENCE, NC, NBOX, NBOX, NBOX)
    spectrum = jnp.fft.fftn(field, axes=(2, 3, 4), norm="ortho").reshape(WINDOW_VALENCE, NC, GRID_POINTS)
    picked = spectrum[:, :, sphere_index]
    values = jnp.stack([jnp.real(picked), jnp.imag(picked)], axis=2).astype(jnp.float32)
    plain = values.astype(jnp.bfloat16).reshape(WINDOW_VALENCE * NC, 2, NG)
    scaled = (weights[:, :, None, None] * values).astype(jnp.bfloat16).reshape(WINDOW_VALENCE * NC, 2, NG)
    left = jnp.transpose(scaled, (1, 0, 2)).reshape(2 * WINDOW_VALENCE * NC, NG)
    right = jnp.transpose(plain, (1, 0, 2)).reshape(2 * WINDOW_VALENCE * NC, NG)
    real_part = jnp.dot(left.T, right, preferred_element_type=jnp.float32)
    imag_part = jnp.dot(scaled[:, 1].T, plain[:, 0], preferred_element_type=jnp.float32) - jnp.dot(scaled[:, 0].T, plain[:, 1], preferred_element_type=jnp.float32)
    return jnp.stack([real_part, imag_part])
```

```python
import functools
import math

import jax
import jax.numpy as jnp
import ml_dtypes
import numpy as np
from jax import lax
from jax.experimental import pallas as pl
from jax.experimental.pallas import tpu as pltpu
from jax.sharding import PartitionSpec as P

NBOX = 40
RADIX = 4
VMEM = 56 * 1024 * 1024
BF = jnp.bfloat16
F32 = jnp.float32


def split_host(table):
    high = table.astype(np.float32).astype(ml_dtypes.bfloat16)
    low = (table - high.astype(np.float64)).astype(ml_dtypes.bfloat16)
    return np.stack([high, low])


def host_tables(count, pairs):
    square = count * count
    part = square // RADIX
    wide = -(-part // 128) * 128
    rows = np.arange(part)
    tables = []
    for residue in range(RADIX):
        freq_b = RADIX * (rows // count) + residue
        freq_e = rows % count
        steps = (np.outer(rows // count, freq_b) + np.outer(rows % count, freq_e)) % count
        angle = 2.0 * math.pi / count * steps
        both = np.zeros((2, part, wide))
        both[0, :, :part] = np.cos(angle) / count
        both[1, :, :part] = np.sin(angle) / count
        tables.append(split_host(both))
    plane = np.stack(tables)
    line = np.arange(count)
    angle = 2.0 * math.pi / count * (np.outer(line, line) % count)
    cosine, sine = np.cos(angle) / math.sqrt(count), np.sin(angle) / math.sqrt(count)
    first = np.zeros((count, 2, pairs, 2, pairs, count))
    for pair in range(pairs):
        first[:, 0, pair, 0, pair] = cosine
        first[:, 0, pair, 1, pair] = sine
        first[:, 1, pair, 0, pair] = -sine
        first[:, 1, pair, 1, pair] = cosine
    size = 2 * pairs * count
    return plane, split_host(first.reshape(size, size)), part, wide


def dft_kernel(nbands, count, val_ref, con_ref, plane_ref, first_ref, out_ref, x_ref):
    step = pl.program_id(0)
    half = x_ref.shape[1] // 2
    block = con_ref.shape[2]
    bands = block // count

    @pl.when(step == 0)
    def _():
        for band in range(nbands):
            re, im = [], []
            for quarter in range(RADIX):
                con_re = con_ref[0, quarter].astype(F32)
                con_im = con_ref[1, quarter].astype(F32)
                own = slice(band * count, (band + 1) * count)
                val_re = val_ref[0, quarter].astype(F32)[own]
                val_im = val_ref[1, quarter].astype(F32)[own]
                val_re = jnp.concatenate([val_re] * bands, axis=0)
                val_im = jnp.concatenate([val_im] * bands, axis=0)
                re.append(val_re * con_re + val_im * con_im)
                im.append(val_re * con_im - val_im * con_re)
            a_re, a_im = re[0] + re[2], im[0] + im[2]
            b_re, b_im = re[0] - re[2], im[0] - im[2]
            c_re, c_im = re[1] + re[3], im[1] + im[3]
            d_re, d_im = re[1] - re[3], im[1] - im[3]
            made = [
                (a_re + c_re, a_im + c_im),
                (b_re + d_im, b_im - d_re),
                (a_re - c_re, a_im - c_im),
                (b_re - d_im, b_im + d_re),
            ]
            for residue in range(RADIX):
                for comp in range(2):
                    value = made[residue][comp]
                    high = value.astype(BF)
                    low = (value - high.astype(F32)).astype(BF)
                    at = comp * (half // 2) + band * block
                    x_ref[residue, at : at + block] = high
                    x_ref[residue, half + at : half + at + block] = low

    dot = functools.partial(jnp.dot, preferred_element_type=F32)
    x = x_ref[step]

    def accurate(which):
        main = dot(x, plane_ref[0, 0, which])
        return main[:half] + main[half:] + dot(x[:half], plane_ref[0, 1, which])

    cos_part = accurate(0)
    sin_part = accurate(1)
    quart = half // 2
    planes = jnp.concatenate(
        [cos_part[:quart] + sin_part[quart:], cos_part[quart:] - sin_part[:quart]], axis=0
    )
    high = planes.astype(BF)
    low = (planes - high.astype(F32)).astype(BF)
    total = dot(first_ref[0], high) + dot(first_ref[0], low) + dot(first_ref[1], high)
    out_ref[...] = total.astype(BF)


def pick_kernel(count, spec_ref, plane_at_ref, first_at_ref, weight_ref, plain_ref, scaled_ref):
    rows, depth = spec_ref.shape
    comps = rows // count
    place = plane_at_ref[0]
    width = place.shape[-1]
    total = jnp.zeros((rows, width), F32)
    chunk = 256 if depth % 256 == 0 else 128
    ident = lax.broadcasted_iota(jnp.int32, (chunk, width), 0)
    for start in range(0, depth, chunk):
        hot = jnp.where(ident == place - start, 1.0, 0.0).astype(BF)
        total += jnp.dot(spec_ref[:, start : start + chunk], hot, preferred_element_type=F32)
    freq = jnp.broadcast_to(first_at_ref[0], (comps, width))
    value = jnp.zeros((comps, width), F32)
    for k in range(count):
        value += jnp.where(freq == k, total[k * comps : (k + 1) * comps], 0.0)
    plain_ref[0] = value.astype(BF)
    scaled_ref[0] = (weight_ref[...] * value).astype(BF)


def outer_kernel(left_ref, right_ref, turned_ref, out_ref):
    left = left_ref[...]
    width = out_ref.shape[-1]
    out_ref[0] = jnp.dot(left, right_ref[...], preferred_element_type=F32)[:, :width]
    out_ref[1] = jnp.dot(left, turned_ref[...], preferred_element_type=F32)[:, :width]


def params(**kw):
    return pltpu.CompilerParams(vmem_limit_bytes=VMEM, **kw)


def largest(total, unit, most):
    return max(t for t in range(unit, most + 1, unit) if total % t == 0)


def on_device(valence, conduction, valence_slot_index, weights, sphere_index):
    rows = lax.axis_size("row")
    cols = lax.axis_size("col")
    nbands, nown = weights.shape
    pairs = nbands * nown
    count = NBOX
    square = count * count
    plane, first, part, wide = host_tables(count, pairs)

    def arrange(x):
        n = x.shape[0]
        x = x.reshape(n, 2, count, RADIX, part)
        return jnp.transpose(x, (1, 3, 0, 2, 4)).reshape(2, RADIX, n * count, part)

    stored = arrange(valence).reshape(2, RADIX, 1, count, part)
    me = lax.axis_index("row") * cols + lax.axis_index("col")
    mine = (valence_slot_index == me).reshape(1, 1, nbands, 1, 1)
    chosen = lax.psum(jnp.where(mine, stored, jnp.zeros_like(stored)), ("row", "col"))
    chosen = chosen.reshape(2, RADIX, nbands * count, part)
    states = arrange(conduction)

    size = 2 * pairs * count
    spectrum = pl.pallas_call(
        functools.partial(dft_kernel, nbands, count),
        grid=(RADIX,),
        in_specs=[
            pl.BlockSpec(chosen.shape, lambda r: (0, 0, 0, 0)),
            pl.BlockSpec(states.shape, lambda r: (0, 0, 0, 0)),
            pl.BlockSpec((1,) + plane.shape[1:], lambda r: (r, 0, 0, 0, 0)),
            pl.BlockSpec(first.shape, lambda r: (0, 0, 0)),
        ],
        out_specs=pl.BlockSpec((size, wide), lambda r: (0, r)),
        out_shape=jax.ShapeDtypeStruct((size, RADIX * wide), BF),
        scratch_shapes=[pltpu.VMEM((RADIX, 2 * size, part), BF)],
        compiler_params=params(),
    )(chosen, states, jnp.asarray(plane), jnp.asarray(first))

    ng = sphere_index.shape[0]
    unit = ng // cols
    unit_wide = -(-unit // 128) * 128
    tile = largest(unit_wide, 128, 256)
    freq_b = (sphere_index // count) % count
    place = (freq_b % RADIX) * wide + (freq_b // RADIX) * count + sphere_index % count
    pad = ((0, 0), (0, unit_wide - unit))
    place = jnp.pad(place.reshape(cols, unit), pad, constant_values=-1)[:, None]
    leading = jnp.pad((sphere_index // square).reshape(cols, unit), pad)[:, None]
    weight = jnp.tile(weights.reshape(pairs), 2)[:, None]
    shape = jax.ShapeDtypeStruct((cols, 2 * pairs, unit_wide), BF)
    index_spec = pl.BlockSpec((1, 1, tile), lambda u, t: (u, 0, t))
    value_spec = pl.BlockSpec((1, 2 * pairs, tile), lambda u, t: (u, 0, t))
    plain, scaled = pl.pallas_call(
        functools.partial(pick_kernel, count),
        grid=(cols, unit_wide // tile),
        in_specs=[
            pl.BlockSpec(spectrum.shape, lambda u, t: (0, 0)),
            index_spec,
            index_spec,
            pl.BlockSpec(weight.shape, lambda u, t: (0, 0)),
        ],
        out_specs=[value_spec, value_spec],
        out_shape=[shape, shape],
        compiler_params=params(),
    )(spectrum, place, leading, weight)

    per_row = cols // rows
    scaled = scaled.reshape(rows, per_row, 2 * pairs, unit_wide)
    regrouped = lax.all_to_all(scaled, "row", split_axis=0, concat_axis=0, tiled=True)
    row_block = lax.all_gather(regrouped, "col", axis=0)
    spread = lax.all_to_all(plain, "col", split_axis=0, concat_axis=0, tiled=True)
    right = lax.all_gather(spread, "row", axis=0)
    depth = rows * cols * 2 * pairs
    left = jnp.transpose(row_block[..., :unit], (2, 4, 1, 0, 3)).reshape(per_row * unit, depth)
    turned = jnp.concatenate([-right[:, :, pairs:], right[:, :, :pairs]], axis=2)
    right = right.reshape(depth, unit_wide)
    turned = turned.reshape(depth, unit_wide)
    nrows = per_row * unit
    high = largest(nrows, 16, 256)
    return pl.pallas_call(
        outer_kernel,
        grid=(nrows // high,),
        in_specs=[
            pl.BlockSpec((high, depth), lambda i: (i, 0)),
            pl.BlockSpec(right.shape, lambda i: (0, 0)),
            pl.BlockSpec(turned.shape, lambda i: (0, 0)),
        ],
        out_specs=pl.BlockSpec((2, high, unit), lambda i: (0, i, 0)),
        out_shape=jax.ShapeDtypeStruct((2, nrows, unit), F32),
        compiler_params=params(),
    )(left, right, turned)


def solution(mesh):
    placed = (
        P(("row", "col"), None, None),
        P(("row", "col"), None, None),
        P(),
        P(None, ("row", "col")),
        P(),
    )
    return jax.shard_map(
        on_device, mesh=mesh, in_specs=placed, out_specs=P(None, "row", "col"), check_vma=False
    )
```

```python
import functools
import math

import jax
import jax.numpy as jnp
import ml_dtypes
import numpy as np
from jax import lax
from jax.experimental import pallas as pl
from jax.experimental.pallas import tpu as pltpu
from jax.sharding import PartitionSpec as P

NBOX = 40
RADIX = 4
VMEM = 56 * 1024 * 1024
BF = jnp.bfloat16
F32 = jnp.float32


def split_host(table):
    high = table.astype(np.float32).astype(ml_dtypes.bfloat16)
    low = (table - high.astype(np.float64)).astype(ml_dtypes.bfloat16)
    return np.stack([high, low])


def host_tables(count, pairs):
    square = count * count
    part = square // RADIX
    wide = -(-part // 128) * 128
    rows = np.arange(part)
    tables = []
    for residue in range(RADIX):
        freq_b = RADIX * (rows // count) + residue
        freq_e = rows % count
        steps = (np.outer(rows // count, freq_b) + np.outer(rows % count, freq_e)) % count
        angle = 2.0 * math.pi / count * steps
        both = np.zeros((2, part, wide))
        both[0, :, :part] = np.cos(angle) / count
        both[1, :, :part] = np.sin(angle) / count
        tables.append(split_host(both))
    plane = np.stack(tables)
    line = np.arange(count)
    angle = 2.0 * math.pi / count * (np.outer(line, line) % count)
    cosine, sine = np.cos(angle) / math.sqrt(count), np.sin(angle) / math.sqrt(count)
    first = np.zeros((count, 2, pairs, 2, pairs, count))
    for pair in range(pairs):
        first[:, 0, pair, 0, pair] = cosine
        first[:, 0, pair, 1, pair] = sine
        first[:, 1, pair, 0, pair] = -sine
        first[:, 1, pair, 1, pair] = cosine
    size = 2 * pairs * count
    return plane, split_host(first.reshape(size, size)), part, wide


def dft_kernel(nbands, count, val_ref, con_ref, plane_ref, first_ref, out_ref, x_ref):
    step = pl.program_id(0)
    half = x_ref.shape[1] // 2
    block = con_ref.shape[2]
    bands = block // count

    @pl.when(step == 0)
    def _():
        for band in range(nbands):
            re, im = [], []
            for quarter in range(RADIX):
                con_re = con_ref[0, quarter].astype(F32)
                con_im = con_ref[1, quarter].astype(F32)
                own = slice(band * count, (band + 1) * count)
                val_re = val_ref[0, quarter].astype(F32)[own]
                val_im = val_ref[1, quarter].astype(F32)[own]
                val_re = jnp.concatenate([val_re] * bands, axis=0)
                val_im = jnp.concatenate([val_im] * bands, axis=0)
                re.append(val_re * con_re + val_im * con_im)
                im.append(val_re * con_im - val_im * con_re)
            a_re, a_im = re[0] + re[2], im[0] + im[2]
            b_re, b_im = re[0] - re[2], im[0] - im[2]
            c_re, c_im = re[1] + re[3], im[1] + im[3]
            d_re, d_im = re[1] - re[3], im[1] - im[3]
            made = [
                (a_re + c_re, a_im + c_im),
                (b_re + d_im, b_im - d_re),
                (a_re - c_re, a_im - c_im),
                (b_re - d_im, b_im + d_re),
            ]
            for residue in range(RADIX):
                for comp in range(2):
                    value = made[residue][comp]
                    high = value.astype(BF)
                    low = (value - high.astype(F32)).astype(BF)
                    at = comp * (half // 2) + band * block
                    x_ref[residue, at : at + block] = high
                    x_ref[residue, half + at : half + at + block] = low

    dot = functools.partial(jnp.dot, preferred_element_type=F32)
    x = x_ref[step]

    def accurate(which):
        main = dot(x, plane_ref[0, 0, which])
        return main[:half] + main[half:] + dot(x[:half], plane_ref[0, 1, which])

    cos_part = accurate(0)
    sin_part = accurate(1)
    quart = half // 2
    planes = jnp.concatenate(
        [cos_part[:quart] + sin_part[quart:], cos_part[quart:] - sin_part[:quart]], axis=0
    )
    high = planes.astype(BF)
    low = (planes - high.astype(F32)).astype(BF)
    total = dot(first_ref[0], high) + dot(first_ref[0], low) + dot(first_ref[1], high)
    out_ref[...] = total.astype(BF)


def pick_kernel(count, spec_ref, plane_at_ref, first_at_ref, weight_ref, plain_ref, scaled_ref):
    rows, depth = spec_ref.shape
    comps = rows // count
    width = plane_at_ref.shape[-1]
    tile = largest(width, 128, 256)
    ident = lax.broadcasted_iota(jnp.int32, (depth, tile), 0)
    for start in range(0, width, tile):
        at = slice(start, start + tile)
        hot = jnp.where(ident == plane_at_ref[0, :, at], 1.0, 0.0).astype(BF)
        total = jnp.dot(spec_ref[...], hot, preferred_element_type=F32)
        freq = jnp.broadcast_to(first_at_ref[0, :, at], (comps, tile))
        value = jnp.zeros((comps, tile), F32)
        for k in range(count):
            value += jnp.where(freq == k, total[k * comps : (k + 1) * comps], 0.0)
        plain_ref[0, :, at] = value.astype(BF)
        scaled_ref[0, :, at] = (weight_ref[...] * value).astype(BF)


def outer_kernel(left_ref, right_ref, out_ref, left_at, right_at, turned_at):
    rows, cols, comps, _ = right_ref.shape
    high, width = out_ref.shape[1:]
    step = pl.program_id(1)

    @pl.when((pl.program_id(0) == 0) & (step == 0))
    def _():
        for col in range(cols):
            for row in range(rows):
                at = slice((col * rows + row) * comps, (col * rows + row + 1) * comps)
                value = right_ref[row, col]
                right_at[at] = value
                wide = value.astype(F32)
                half = comps // 2
                turned = jnp.concatenate([-wide[half:], wide[:half]], axis=0)
                turned_at[at] = turned.astype(BF)

    @pl.when(step == 0)
    def _():
        left = left_ref[...]
        left_at[...] = left.reshape(-1, left.shape[-1]).T

    left = left_at[pl.ds(pl.multiple_of(step * high, 16), high)]
    out_ref[0] = jnp.dot(left, right_at[...], preferred_element_type=F32)[:, :width]
    out_ref[1] = jnp.dot(left, turned_at[...], preferred_element_type=F32)[:, :width]


def params(**kw):
    return pltpu.CompilerParams(vmem_limit_bytes=VMEM, **kw)


def largest(total, unit, most):
    return max(t for t in range(unit, most + 1, unit) if total % t == 0)


def on_device(valence, conduction, valence_slot_index, weights, sphere_index):
    rows = lax.axis_size("row")
    cols = lax.axis_size("col")
    nbands, nown = weights.shape
    pairs = nbands * nown
    count = NBOX
    square = count * count
    plane, first, part, wide = host_tables(count, pairs)

    def arrange(x):
        n = x.shape[0]
        x = x.reshape(n, 2, count, RADIX, part)
        return jnp.transpose(x, (1, 3, 0, 2, 4)).reshape(2, RADIX, n * count, part)

    me = lax.axis_index("row") * cols + lax.axis_index("col")
    bands = []
    for band in range(nbands):
        mine = jnp.where(valence_slot_index[band] == me, valence[0], jnp.zeros_like(valence[0]))
        bands.append(lax.psum(mine, ("row", "col")))
    bands = lax.optimization_barrier(bands)
    chosen = arrange(jnp.stack(bands))
    states = arrange(conduction)

    size = 2 * pairs * count
    spectrum = pl.pallas_call(
        functools.partial(dft_kernel, nbands, count),
        grid=(RADIX,),
        in_specs=[
            pl.BlockSpec(chosen.shape, lambda r: (0, 0, 0, 0)),
            pl.BlockSpec(states.shape, lambda r: (0, 0, 0, 0)),
            pl.BlockSpec((1,) + plane.shape[1:], lambda r: (r, 0, 0, 0, 0)),
            pl.BlockSpec(first.shape, lambda r: (0, 0, 0)),
        ],
        out_specs=pl.BlockSpec((size, wide), lambda r: (0, r)),
        out_shape=jax.ShapeDtypeStruct((size, RADIX * wide), BF),
        scratch_shapes=[pltpu.VMEM((RADIX, 2 * size, part), BF)],
        compiler_params=params(),
    )(chosen, states, jnp.asarray(plane), jnp.asarray(first))

    ng = sphere_index.shape[0]
    unit = ng // cols
    unit_wide = -(-unit // 128) * 128
    freq_b = (sphere_index // count) % count
    place = (freq_b % RADIX) * wide + (freq_b // RADIX) * count + sphere_index % count
    pad = ((0, 0), (0, unit_wide - unit))
    place = jnp.pad(place.reshape(cols, unit), pad, constant_values=-1)[:, None]
    leading = jnp.pad((sphere_index // square).reshape(cols, unit), pad)[:, None]
    weight = jnp.tile(weights.reshape(pairs), 2)[:, None]
    shape = jax.ShapeDtypeStruct((cols, 2 * pairs, unit_wide), BF)
    index_spec = pl.BlockSpec((1, 1, unit_wide), lambda u: (u, 0, 0))
    value_spec = pl.BlockSpec((1, 2 * pairs, unit_wide), lambda u: (u, 0, 0))
    plain, scaled = pl.pallas_call(
        functools.partial(pick_kernel, count),
        grid=(cols,),
        in_specs=[
            pl.BlockSpec(spectrum.shape, lambda u: (0, 0)),
            index_spec,
            index_spec,
            pl.BlockSpec(weight.shape, lambda u: (0, 0)),
        ],
        out_specs=[value_spec, value_spec],
        out_shape=[shape, shape],
        compiler_params=params(),
    )(spectrum, place, leading, weight)

    per_row = cols // rows
    scaled = scaled.reshape(rows, per_row, 2 * pairs, unit_wide)
    regrouped = lax.all_to_all(scaled, "row", split_axis=0, concat_axis=0, tiled=True)
    row_block = lax.all_gather(regrouped, "col", axis=0)
    spread = lax.all_to_all(plain, "col", split_axis=0, concat_axis=0, tiled=True)
    right = lax.all_gather(spread, "row", axis=0)
    depth = rows * cols * 2 * pairs
    high = largest(unit, 16, 256)
    tiles = unit // high
    return pl.pallas_call(
        outer_kernel,
        grid=(per_row, tiles),
        in_specs=[
            pl.BlockSpec(
                (cols, rows, None, 2 * pairs, unit_wide), lambda u, i: (0, 0, u, 0, 0)
            ),
            pl.BlockSpec(right.shape, lambda u, i: (0, 0, 0, 0)),
        ],
        out_specs=pl.BlockSpec((2, high, unit), lambda u, i: (0, u * tiles + i, 0)),
        out_shape=jax.ShapeDtypeStruct((2, per_row * unit, unit), F32),
        scratch_shapes=[
            pltpu.VMEM((unit_wide, depth), BF),
            pltpu.VMEM((depth, unit_wide), BF),
            pltpu.VMEM((depth, unit_wide), BF),
        ],
        compiler_params=params(),
    )(row_block, right)


def solution(mesh):
    placed = (
        P(("row", "col"), None, None),
        P(("row", "col"), None, None),
        P(),
        P(None, ("row", "col")),
        P(),
    )
    return jax.shard_map(
        on_device, mesh=mesh, in_specs=placed, out_specs=P(None, "row", "col"), check_vma=False
    )
```

```python
import functools
import math

import jax
import jax.numpy as jnp
import ml_dtypes
import numpy as np
from jax import lax
from jax.experimental import pallas as pl
from jax.experimental.pallas import tpu as pltpu
from jax.sharding import PartitionSpec as P

NBOX = 40
RADIX = 4
VMEM = 56 * 1024 * 1024
BF = jnp.bfloat16
F32 = jnp.float32


def split_host(table):
    high = table.astype(np.float32).astype(ml_dtypes.bfloat16)
    low = (table - high.astype(np.float64)).astype(ml_dtypes.bfloat16)
    return np.stack([high, low])


def host_tables(count, pairs):
    square = count * count
    part = square // RADIX
    wide = -(-part // 128) * 128
    rows = np.arange(part)
    tables = []
    for residue in range(RADIX):
        freq_b = RADIX * (rows // count) + residue
        freq_e = rows % count
        steps = (np.outer(rows // count, freq_b) + np.outer(rows % count, freq_e)) % count
        angle = 2.0 * math.pi / count * steps
        both = np.zeros((2, part, wide))
        both[0, :, :part] = np.cos(angle) / count
        both[1, :, :part] = np.sin(angle) / count
        tables.append(split_host(both))
    plane = np.stack(tables)
    line = np.arange(count)
    angle = 2.0 * math.pi / count * (np.outer(line, line) % count)
    cosine, sine = np.cos(angle) / math.sqrt(count), np.sin(angle) / math.sqrt(count)
    first = np.zeros((count, 2, pairs, 2, pairs, count))
    for pair in range(pairs):
        first[:, 0, pair, 0, pair] = cosine
        first[:, 0, pair, 1, pair] = sine
        first[:, 1, pair, 0, pair] = -sine
        first[:, 1, pair, 1, pair] = cosine
    size = 2 * pairs * count
    return plane, split_host(first.reshape(size, size)), part, wide


def dft_kernel(nbands, count, val_ref, con_ref, plane_ref, first_ref, out_ref, x_ref):
    step = pl.program_id(0)
    half = x_ref.shape[1] // 2
    block = con_ref.shape[2]
    bands = block // count

    @pl.when(step == 0)
    def _():
        for band in range(nbands):
            re, im = [], []
            for quarter in range(RADIX):
                con_re = con_ref[0, quarter].astype(F32)
                con_im = con_ref[1, quarter].astype(F32)
                own = slice(band * count, (band + 1) * count)
                val_re = val_ref[0, quarter].astype(F32)[own]
                val_im = val_ref[1, quarter].astype(F32)[own]
                val_re = jnp.concatenate([val_re] * bands, axis=0)
                val_im = jnp.concatenate([val_im] * bands, axis=0)
                re.append(val_re * con_re + val_im * con_im)
                im.append(val_re * con_im - val_im * con_re)
            a_re, a_im = re[0] + re[2], im[0] + im[2]
            b_re, b_im = re[0] - re[2], im[0] - im[2]
            c_re, c_im = re[1] + re[3], im[1] + im[3]
            d_re, d_im = re[1] - re[3], im[1] - im[3]
            made = [
                (a_re + c_re, a_im + c_im),
                (b_re + d_im, b_im - d_re),
                (a_re - c_re, a_im - c_im),
                (b_re - d_im, b_im + d_re),
            ]
            for residue in range(RADIX):
                for comp in range(2):
                    value = made[residue][comp]
                    high = value.astype(BF)
                    low = (value - high.astype(F32)).astype(BF)
                    at = comp * (half // 2) + band * block
                    x_ref[residue, at : at + block] = high
                    x_ref[residue, half + at : half + at + block] = low

    dot = functools.partial(jnp.dot, preferred_element_type=F32)
    x = x_ref[step]

    def accurate(which):
        main = dot(x, plane_ref[0, 0, which])
        return main[:half] + main[half:] + dot(x[:half], plane_ref[0, 1, which])

    cos_part = accurate(0)
    sin_part = accurate(1)
    quart = half // 2
    planes = jnp.concatenate(
        [cos_part[:quart] + sin_part[quart:], cos_part[quart:] - sin_part[:quart]], axis=0
    )
    high = planes.astype(BF)
    low = (planes - high.astype(F32)).astype(BF)
    total = dot(first_ref[0], high) + dot(first_ref[0], low) + dot(first_ref[1], high)
    out_ref[...] = total.astype(BF)


def pick_kernel(count, spec_ref, plane_at_ref, first_at_ref, weight_ref, plain_ref, scaled_ref):
    rows, depth = spec_ref.shape
    comps = rows // count
    width = plane_at_ref.shape[-1]
    tile = largest(width, 128, 256)
    ident = lax.broadcasted_iota(jnp.int32, (depth, tile), 0)
    for start in range(0, width, tile):
        at = slice(start, start + tile)
        hot = jnp.where(ident == plane_at_ref[0, :, at], 1.0, 0.0).astype(BF)
        total = jnp.dot(spec_ref[...], hot, preferred_element_type=F32)
        freq = jnp.broadcast_to(first_at_ref[0, :, at], (comps, tile))
        value = jnp.zeros((comps, tile), F32)
        for k in range(count):
            value += jnp.where(freq == k, total[k * comps : (k + 1) * comps], 0.0)
        plain_ref[0, :, at] = value.astype(BF)
        scaled_ref[0, :, at] = (weight_ref[...] * value).astype(BF)


def outer_kernel(here_ref, left_ref, right_ref, out_ref, left_at, right_at, turned_at):
    rows, cols, comps, _ = right_ref.shape
    high, width = out_ref.shape[1:]
    step = pl.program_id(1)

    @pl.when((pl.program_id(0) == 0) & (step == 0))
    def _():
        for col in range(cols):
            for row in range(rows):
                at = slice((col * rows + row) * comps, (col * rows + row + 1) * comps)
                value = right_ref[lax.rem(here_ref[0] + rows - row, rows), col]
                right_at[at] = value
                wide = value.astype(F32)
                half = comps // 2
                turned = jnp.concatenate([-wide[half:], wide[:half]], axis=0)
                turned_at[at] = turned.astype(BF)

    @pl.when(step == 0)
    def _():
        left = left_ref[...]
        left_at[...] = left.reshape(-1, left.shape[-1]).T

    left = left_at[pl.ds(pl.multiple_of(step * high, 16), high)]
    out_ref[0] = jnp.dot(left, right_at[...], preferred_element_type=F32)[:, :width]
    out_ref[1] = jnp.dot(left, turned_at[...], preferred_element_type=F32)[:, :width]


def params(**kw):
    return pltpu.CompilerParams(vmem_limit_bytes=VMEM, **kw)


def largest(total, unit, most):
    return max(t for t in range(unit, most + 1, unit) if total % t == 0)


def on_device(valence, conduction, valence_slot_index, weights, sphere_index):
    rows = lax.axis_size("row")
    cols = lax.axis_size("col")
    nbands, nown = weights.shape
    pairs = nbands * nown
    count = NBOX
    square = count * count
    plane, first, part, wide = host_tables(count, pairs)

    def arrange(x):
        n = x.shape[0]
        x = x.reshape(n, 2, count, RADIX, part)
        return jnp.transpose(x, (1, 3, 0, 2, 4)).reshape(2, RADIX, n * count, part)

    me = lax.axis_index("row") * cols + lax.axis_index("col")
    points = valence.shape[-1]
    lines = nbands * 2 * points // 128
    share = -(-lines // (cols * 16)) * 16
    stored = valence.reshape(1, 2, points // 128, 128)
    mine = (valence_slot_index == me).reshape(nbands, 1, 1, 1)
    blocks = jnp.where(mine, stored, jnp.zeros_like(stored)).reshape(lines, 128)
    blocks = jnp.pad(blocks, ((0, cols * share - lines), (0, 0))).reshape(cols, share, 128)
    blocks = lax.all_to_all(blocks, "col", split_axis=0, concat_axis=0, tiled=True)
    block = jnp.sum(blocks, axis=0, dtype=F32).astype(BF)
    block = jnp.sum(lax.all_gather(block, "row", axis=0), axis=0, dtype=F32).astype(BF)
    bands = lax.all_gather(block, "col", axis=0, tiled=True)
    bands = lax.optimization_barrier(bands)
    chosen = arrange(bands[:lines].reshape(nbands, 2, points))
    states = arrange(conduction)

    size = 2 * pairs * count
    spectrum = pl.pallas_call(
        functools.partial(dft_kernel, nbands, count),
        grid=(RADIX,),
        in_specs=[
            pl.BlockSpec(chosen.shape, lambda r: (0, 0, 0, 0)),
            pl.BlockSpec(states.shape, lambda r: (0, 0, 0, 0)),
            pl.BlockSpec((1,) + plane.shape[1:], lambda r: (r, 0, 0, 0, 0)),
            pl.BlockSpec(first.shape, lambda r: (0, 0, 0)),
        ],
        out_specs=pl.BlockSpec((size, wide), lambda r: (0, r)),
        out_shape=jax.ShapeDtypeStruct((size, RADIX * wide), BF),
        scratch_shapes=[pltpu.VMEM((RADIX, 2 * size, part), BF)],
        compiler_params=params(),
    )(chosen, states, jnp.asarray(plane), jnp.asarray(first))

    ng = sphere_index.shape[0]
    unit = ng // cols
    unit_wide = -(-unit // 128) * 128
    freq_b = (sphere_index // count) % count
    place = (freq_b % RADIX) * wide + (freq_b // RADIX) * count + sphere_index % count
    pad = ((0, 0), (0, unit_wide - unit))
    place = jnp.pad(place.reshape(cols, unit), pad, constant_values=-1)[:, None]
    leading = jnp.pad((sphere_index // square).reshape(cols, unit), pad)[:, None]
    weight = jnp.tile(weights.reshape(pairs), 2)[:, None]
    shape = jax.ShapeDtypeStruct((cols, 2 * pairs, unit_wide), BF)
    index_spec = pl.BlockSpec((1, 1, unit_wide), lambda u: (u, 0, 0))
    value_spec = pl.BlockSpec((1, 2 * pairs, unit_wide), lambda u: (u, 0, 0))
    plain, scaled = pl.pallas_call(
        functools.partial(pick_kernel, count),
        grid=(cols,),
        in_specs=[
            pl.BlockSpec(spectrum.shape, lambda u: (0, 0)),
            index_spec,
            index_spec,
            pl.BlockSpec(weight.shape, lambda u: (0, 0)),
        ],
        out_specs=[value_spec, value_spec],
        out_shape=[shape, shape],
        compiler_params=params(),
    )(spectrum, place, leading, weight)

    per_row = cols // rows
    scaled = scaled.reshape(rows, per_row, 2 * pairs, unit_wide)
    here = lax.axis_index("row")
    parts = []
    for shift in range(rows):
        part_out = lax.dynamic_index_in_dim(scaled, (here + shift) % rows, 0, keepdims=False)
        if shift > 0:
            hops = [(row, (row + shift) % rows) for row in range(rows)]
            part_out = lax.ppermute(part_out, "row", hops)
        parts.append(part_out)
    regrouped = jnp.stack(parts)
    row_block = lax.all_gather(regrouped, "col", axis=0)
    spread = lax.all_to_all(plain, "col", split_axis=0, concat_axis=0, tiled=True)
    right = lax.all_gather(spread, "row", axis=0)
    depth = rows * cols * 2 * pairs
    high = largest(unit, 16, 256)
    tiles = unit // high
    return pl.pallas_call(
        outer_kernel,
        grid=(per_row, tiles),
        in_specs=[
            pl.BlockSpec(memory_space=pltpu.SMEM),
            pl.BlockSpec(
                (cols, rows, None, 2 * pairs, unit_wide), lambda u, i: (0, 0, u, 0, 0)
            ),
            pl.BlockSpec(right.shape, lambda u, i: (0, 0, 0, 0)),
        ],
        out_specs=pl.BlockSpec((2, high, unit), lambda u, i: (0, u * tiles + i, 0)),
        out_shape=jax.ShapeDtypeStruct((2, per_row * unit, unit), F32),
        scratch_shapes=[
            pltpu.VMEM((unit_wide, depth), BF),
            pltpu.VMEM((depth, unit_wide), BF),
            pltpu.VMEM((depth, unit_wide), BF),
        ],
        compiler_params=params(),
    )(here.astype(jnp.int32).reshape(1), row_block, right)


def solution(mesh):
    placed = (
        P(("row", "col"), None, None),
        P(("row", "col"), None, None),
        P(),
        P(None, ("row", "col")),
        P(),
    )
    return jax.shard_map(
        on_device, mesh=mesh, in_specs=placed, out_specs=P(None, "row", "col"), check_vma=False
    )
```
